128 devices in a mesh: store: 8 (over y, x_lo), ctx: 8 (over z, core), head: 2 (over x_hi).
Axes of the slice: x: 4 (x_hi: 2, x_lo: 2; x = x_hi * 2 + x_lo), y: 4, z: 4, core: 2. Of those that a mesh axis runs over, the one named last changes fastest.
Arguments:
- queries: bfloat16 [8192, 4096], P(('store', 'ctx'), 'head')
- suffix_hidden: bfloat16 [8192, 8192], P(('store', 'ctx'), 'head'), may hold values from -6 to 6
- prefix_hidden: bfloat16 [8192, 8192], P(('store', 'ctx'), 'head'), may hold values from -6 to 6
- kv_cache: bfloat16 [32, 2, 256, 512], P('store', None, None, 'head')
- counts: int32 [8], replicated, may hold values from 1 to 4, as said below
- w_key: bfloat16 [8192, 512], P('head'), may hold values from -0.0625 to 0.0625
- w_value: bfloat16 [8192, 512], P('head'), may hold values from -0.0625 to 0.0625
Outputs:
- attended: bfloat16 [8192, 4096], P(('store', 'ctx'), 'head')
The draws below stay inside these ranges and needn't reach their ends.
Inputs may be any that keep to these rules, and one draw needn't show every extreme that they name: `counts`: some owner has all 4 slots live and another has one.
All inputs are finite; a program needn't handle non-finite values.
Results may differ from the reference program's by a relative error of at most 0.0098.
Values may be sent and summed in bfloat16 or wider, within the bound.
No kernel may reach another device: no remote copies, remote signals or barrier semaphores. Data moves between devices by JAX's collectives and lax.ppermute only.
A program may use at most 128 MiB of HBM per device.

```python
import math
import jax
import jax.numpy as jnp
from jax import lax

D = 8192
HQ = 32
KVH = 4
HD = 128
BLOCK = 256
SLOTS = 4
SUF = 8192
RECOMP = 8192
N_STORE = 8


def draw_queries(key, part):
    key = jax.random.fold_in(key, 11)
    entries = jnp.clip(3.0 * jax.random.normal(key, (SUF, HQ * HD), jnp.float32), -15.0, 15.0)
    return entries.astype(jnp.bfloat16)


def draw_kv_cache(key, part):
    key = jax.random.fold_in(key, 23)
    key_noise = jax.random.fold_in(key, 0)
    entries = jax.random.normal(key_noise, (N_STORE * SLOTS, 2, BLOCK, KVH * HD), jnp.float32)
    return entries.astype(jnp.bfloat16)


def draw_counts(key, part):
    key = jax.random.fold_in(key, 37)
    key_fill, key_full, key_single = jax.random.split(key, 3)
    filled = jax.random.randint(key_fill, (N_STORE,), 1, SLOTS + 1)
    fullest = jax.random.randint(key_full, (), 0, N_STORE)
    single = (fullest + jax.random.randint(key_single, (), 1, N_STORE)) % N_STORE
    owner_ids = jnp.arange(N_STORE)
    result = jnp.where(owner_ids == single, 1, filled)
    result = jnp.where(owner_ids == fullest, SLOTS, result)
    return result.astype(jnp.int32)


def block_scale(key, dims, shards, low, high):
    loudness, own = 1.0, jax.random.fold_in(key, 6)
    for axis_at, parts in shards:
        heights = jnp.exp(jax.random.uniform(jax.random.fold_in(own, axis_at), (parts,), jnp.float32, low / len(shards), high / len(shards)))
        loudness = loudness * jnp.repeat(heights, dims[axis_at] // parts).reshape([-1 if axis == axis_at else 1 for axis in range(len(dims))])
    return loudness


def scatter_about(key, extent, deviation, limit, cuts=(), kind=jnp.bfloat16):
    values = deviation * jax.random.normal(key, extent, jnp.float32)
    if cuts:
        values = values * block_scale(key, extent, cuts, -0.22, 0.18)
    return jnp.clip(values, -limit, limit).astype(kind)


def setup_inputs(seed: int = 0) -> dict:
    seeds = jax.random.split(jax.random.key(seed), 8)
    return {
        "queries": draw_queries(jax.random.fold_in(seeds[7], 71), 0),
        "suffix_hidden": scatter_about(seeds[1], (SUF, D), 1.0, 6.0, ((0, 64), (1, 2))),
        "prefix_hidden": scatter_about(seeds[2], (RECOMP, D), 1.0, 6.0, ((0, 64), (1, 2))),
        "kv_cache": draw_kv_cache(jax.random.fold_in(seeds[7], 71), 0),
        "counts": draw_counts(jax.random.fold_in(seeds[7], 71), 0),
        "w_key": scatter_about(seeds[5], (D, KVH * HD), D ** -0.5, 0.0625, ((0, 2),)),
        "w_value": scatter_about(seeds[6], (D, KVH * HD), D ** -0.5, 0.0625, ((0, 2),)),
    }


def reference(queries, suffix_hidden, prefix_hidden, kv_cache, counts, w_key, w_value):
    score_scale = 1.0 / math.sqrt(HD)
    stacked = jnp.concatenate([prefix_hidden, suffix_hidden], axis=0)
    fresh_keys = jnp.dot(stacked, w_key, preferred_element_type=jnp.float32).astype(jnp.bfloat16)
    fresh_values = jnp.dot(stacked, w_value, preferred_element_type=jnp.float32).astype(jnp.bfloat16)
    slot_ids = jnp.arange(N_STORE * SLOTS, dtype=jnp.int32)
    live_slot = slot_ids % SLOTS < counts[slot_ids // SLOTS]
    cached_reach = jnp.repeat(jnp.where(live_slot, -1, 2 ** 30).astype(jnp.int32), BLOCK)
    key_reach = jnp.concatenate([cached_reach, jnp.full((RECOMP,), -1, jnp.int32), jnp.arange(SUF, dtype=jnp.int32)])
    keys_all = jnp.concatenate([kv_cache[:, 0].reshape(-1, KVH * HD), fresh_keys], axis=0)
    values_all = jnp.concatenate([kv_cache[:, 1].reshape(-1, KVH * HD), fresh_values], axis=0)
    keys_all = keys_all.reshape(-1, KVH, HD).astype(jnp.float32)
    values_all = values_all.reshape(-1, KVH, HD).astype(jnp.float32)
    query_block = math.gcd(SUF, 64)

    def one_block(block_index):
        query_rows = lax.dynamic_slice_in_dim(queries, block_index * query_block, query_block, 0)
        grouped = query_rows.reshape(query_block, KVH, HQ // KVH, HD).astype(jnp.float32)
        scores = jnp.einsum('qkgd,nkd->qkgn', grouped, keys_all) * score_scale
        query_pos = block_index * query_block + jnp.arange(query_block, dtype=jnp.int32)
        visible = (key_reach[None, :] <= query_pos[:, None])[:, None, None, :]
        row_max = lax.optimization_barrier(jnp.max(jnp.where(visible, scores, -1e+30), axis=-1, keepdims=True))
        weights = jnp.where(visible, jnp.exp(scores - row_max), 0.0)
        denominator = lax.optimization_barrier(jnp.sum(weights, axis=-1))
        rounded = lax.optimization_barrier(weights.astype(jnp.bfloat16)).astype(jnp.float32)
        attended = jnp.einsum('qkgn,nkd->qkgd', rounded, values_all) / denominator[..., None]
        return attended.reshape(query_block, HQ * HD).astype(jnp.bfloat16)
    blocks = lax.map(one_block, jnp.arange(SUF // query_block, dtype=jnp.int32))
    return blocks.reshape(SUF, HQ * HD)
```

```python
import functools
import math

import jax
import jax.numpy as jnp
from jax import lax
from jax.experimental import pallas as pl
from jax.experimental.pallas import tpu as pltpu
from jax.sharding import PartitionSpec as P

HD = 128
SCALE = math.log2(math.e) / math.sqrt(HD)
SAFE = 2.0**100
F32 = jnp.float32
BF16 = jnp.bfloat16
VMEM_LIMIT = 56 * 2**20


def project_kernel(info, xp, xs, wk, wv, own, own_suffix, other_prefix, other_suffix, acc_k, acc_v, *, rows, steps, half):
    step = pl.program_id(0)

    @pl.when(step == 0)
    def _():
        acc_k[...] = jnp.zeros_like(acc_k)
        acc_v[...] = jnp.zeros_like(acc_v)

    x = jnp.concatenate([xp[...], xs[...]], axis=0)
    acc_k[...] += jnp.dot(x, wk[...], preferred_element_type=F32)
    acc_v[...] += jnp.dot(x, wv[...], preferred_element_type=F32)

    @pl.when(step == steps - 1)
    def _():
        mine = pl.ds(pl.multiple_of(info[4] * half, half), half)
        theirs = pl.ds(pl.multiple_of((1 - info[4]) * half, half), half)
        own[:, :half] = acc_k[:, mine]
        own[:, half:] = acc_v[:, mine]
        own_suffix[:, :half] = acc_k[rows:, mine].astype(BF16)
        own_suffix[:, half:] = acc_v[rows:, mine].astype(BF16)
        other_prefix[:, :half] = acc_k[:rows, theirs].astype(BF16)
        other_prefix[:, half:] = acc_v[:rows, theirs].astype(BF16)
        other_suffix[:, :half] = acc_k[rows:, theirs].astype(BF16)
        other_suffix[:, half:] = acc_v[rows:, theirs].astype(BF16)


def project(info, prefix, suffix, w_key, w_value):
    rows, feats = prefix.shape
    cols = w_key.shape[1]
    depth = 1024
    steps = feats // depth
    half = cols // 2
    return pl.pallas_call(
        functools.partial(project_kernel, rows=rows, steps=steps, half=half),
        grid=(steps,),
        in_specs=[
            pl.BlockSpec(memory_space=pltpu.SMEM),
            pl.BlockSpec((rows, depth), lambda i: (0, i)),
            pl.BlockSpec((rows, depth), lambda i: (0, i)),
            pl.BlockSpec((depth, cols), lambda i: (i, 0)),
            pl.BlockSpec((depth, cols), lambda i: (i, 0)),
        ],
        out_specs=[pl.BlockSpec((2 * rows, cols), lambda i: (0, 0))] + [pl.BlockSpec((rows, cols), lambda i: (0, 0))] * 3,
        out_shape=[jax.ShapeDtypeStruct((2 * rows, cols), F32)] + [jax.ShapeDtypeStruct((rows, cols), BF16)] * 3,
        scratch_shapes=[pltpu.VMEM((2 * rows, cols), F32), pltpu.VMEM((2 * rows, cols), F32)],
        compiler_params=pltpu.CompilerParams(vmem_limit_bytes=VMEM_LIMIT),
        cost_estimate=pl.CostEstimate(flops=4 * rows * feats * cols * 2, bytes_accessed=4 * feats * cols + 4 * rows * feats, transcendentals=0),
        name="project",
    )(info, prefix, suffix, w_key, w_value)


def combine_kernel(info, own, prefix, suffix, moved, payload):
    rows, cols = prefix.shape
    half = cols // 2
    stays = (own[rows:, :], moved[...].astype(F32))
    base = jnp.where(info[3] == 1, stays[0], stays[1])
    whole = jnp.concatenate([own[:rows, :] + prefix[...].astype(F32), base + suffix[...].astype(F32)], axis=0).astype(BF16)
    payload[0, : 2 * rows, :] = whole[:, :half]
    payload[0, 2 * rows :, :] = jnp.transpose(whole[:, half:])


def combine(info, own, prefix, suffix, moved):
    rows, cols = own.shape
    return pl.pallas_call(
        combine_kernel,
        in_specs=[pl.BlockSpec(memory_space=pltpu.SMEM)] + [pl.BlockSpec(memory_space=pltpu.VMEM)] * 4,
        out_specs=pl.BlockSpec(memory_space=pltpu.VMEM),
        out_shape=jax.ShapeDtypeStruct((1, rows + cols // 2, cols // 2), BF16),
        name="combine",
    )(info, own, prefix, suffix, moved)


def stack_queries(q, qs):
    for j in range(2):
        for g in range(8):
            h = j * 8 + g
            qs[j, g * 128 : (g + 1) * 128, :] = q[:, h * 128 : (h + 1) * 128]


def scores_of(k, q):
    return lax.dot_general(k, q, (((1,), (1,)), ((), ())), preferred_element_type=F32)


def fast_block(j, k, vt, qs, m, l, acc, bias=None):
    size = k.shape[0]
    s = scores_of(k, qs[j])
    t = s.reshape(size // 8, 8, 1024) * SCALE - m[j][None]
    if bias is not None:
        t = t + jnp.concatenate([bias] * 8, axis=1).reshape(size // 8, 8, 1024)
    p = jnp.exp2(t)
    l[j] += jnp.sum(p, axis=0)
    acc[j] += jnp.dot(vt, p.reshape(size, 1024).astype(BF16), preferred_element_type=F32)


def slow_block(j, k, vt, qs, m, l, acc, bias=None):
    size = k.shape[0]
    s = scores_of(k, qs[j]) * SCALE
    if bias is not None:
        s = s + jnp.concatenate([bias] * 8, axis=1)
    old = m[j]
    top = jnp.broadcast_to(jnp.max(s, axis=0, keepdims=True), (8, 1024))
    new = jnp.maximum(old, top)
    m[j] = new
    shrink = jnp.exp2(old - new)
    p = jnp.exp2(s.reshape(size // 8, 8, 1024) - new[None])
    l[j] = l[j] * shrink + jnp.sum(p, axis=0)
    wide = jnp.broadcast_to(shrink[None], (16, 8, 1024)).reshape(128, 1024)
    acc[j] = acc[j] * wide + jnp.dot(vt, p.reshape(size, 1024).astype(BF16), preferred_element_type=F32)


def is_safe(l, acc):
    top = jnp.max(l[...])
    big = jnp.max(jnp.abs(acc[...]))
    return jnp.logical_and(top < SAFE, big < 1e36)


def head_rows(ref, start, size, j):
    return ref[pl.ds(start, size), j * 128 : (j + 1) * 128]


def cached_kernel(info, counts, q0, q1, q2, q3, mine, same, swapped, m_out, l_out, acc_out, keys, values_t, qs, bias, *, slot_rows):
    step = pl.program_id(0)
    y, x, z, core = info[0], info[1], info[2], info[3]
    owner, partner = 2 * y + x, 2 * y + 1 - x
    live = counts[owner] + counts[partner]

    @pl.when(step == 0)
    def _():
        keys[...] = jnp.zeros_like(keys)
        values_t[...] = jnp.zeros_like(values_t)
        slots = [(mine.at[t], t < counts[owner]) for t in range(4)]
        slots += [(same.at[t], 2 * core + t < counts[partner]) for t in range(2)]
        slots += [(swapped.at[t], 2 * (1 - core) + t < counts[partner]) for t in range(2)]
        at = jnp.int32(0)
        for ref, here in slots:
            place = pl.ds(pl.multiple_of(at * slot_rows, slot_rows), slot_rows)

            @pl.when(here)
            def _(place=place, ref=ref):
                keys[place, :] = ref[0]
                values_t[:, place] = jnp.transpose(ref[1])

            at = at + here.astype(jnp.int32)

    for i, q in enumerate((q0, q1, q2, q3)):

        @pl.when(step == i)
        def _(q=q):
            stack_queries(q, qs)

    m, l, acc = m_out.at[0], l_out.at[0], acc_out.at[0]
    used = live * slot_rows
    blocks = (used + 511) // 512
    last = blocks - 1
    row = lax.broadcasted_iota(jnp.int32, (512, 128), 0)
    bias[...] = jnp.where(row + last * 512 < used, 0.0, -jnp.inf)

    for j in range(2):
        s = scores_of(keys[0:256, j * 128 : (j + 1) * 128], qs[j])
        m[j] = jnp.broadcast_to(jnp.max(s, axis=0, keepdims=True), (8, 1024)) * SCALE
    l[...] = jnp.zeros(l.shape, F32)
    acc[...] = jnp.zeros(acc.shape, F32)

    def sweep(block):
        def at(i, b):
            start = pl.multiple_of(i * 512, 512)
            for j in range(2):
                k = head_rows(keys, start, 512, j)
                vt = values_t[j * 128 : (j + 1) * 128, pl.ds(start, 512)]
                block(j, k, vt, qs, m, l, acc, b)

        def body(i, carry):
            at(i, None)
            return carry

        lax.fori_loop(0, last, body, 0)
        at(last, bias[...])

    sweep(fast_block)

    @pl.when(jnp.logical_not(is_safe(l, acc)))
    def _():
        l[...] = jnp.zeros(l.shape, F32)
        acc[...] = jnp.zeros(acc.shape, F32)
        sweep(slow_block)


def attend_cached(info, counts, queries, mine, same, swapped):
    slot_rows = mine.shape[2]
    total = 8 * slot_rows
    rows = queries[0].shape[0]
    whole = pl.BlockSpec(memory_space=pltpu.VMEM)
    smem = pl.BlockSpec(memory_space=pltpu.SMEM)
    return pl.pallas_call(
        functools.partial(cached_kernel, slot_rows=slot_rows),
        grid=(4,),
        in_specs=[smem, smem] + [whole] * 7,
        out_specs=[
            pl.BlockSpec((1, 2, 8, 1024), lambda i: (i, 0, 0, 0)),
            pl.BlockSpec((1, 2, 8, 1024), lambda i: (i, 0, 0, 0)),
            pl.BlockSpec((1, 2, 128, 1024), lambda i: (i, 0, 0, 0)),
        ],
        out_shape=[
            jax.ShapeDtypeStruct((4, 2, 8, 1024), F32),
            jax.ShapeDtypeStruct((4, 2, 8, 1024), F32),
            jax.ShapeDtypeStruct((4, 2, 128, 1024), F32),
        ],
        scratch_shapes=[
            pltpu.VMEM((total, 256), BF16),
            pltpu.VMEM((256, total), BF16),
            pltpu.VMEM((2, 1024, 128), BF16),
            pltpu.VMEM((512, 128), F32),
        ],
        compiler_params=pltpu.CompilerParams(vmem_limit_bytes=VMEM_LIMIT),
        cost_estimate=pl.CostEstimate(flops=4 * 16 * rows * 4 * total * 128, bytes_accessed=16 * 2**20, transcendentals=4 * 16 * rows * total),
        name="attend_cached",
    )(info, counts, *queries, mine, same, swapped)


def fresh_kernel(info, q, m_in, l_in, acc_in, *rest, chunk):
    parts = rest[:8]
    out, keys, values_t, qs, bias, m, l, acc, sem = rest[8:]
    y, x, z, core = info[0], info[1], info[2], info[3]
    copies = [[], [], [], []]
    for n, ref in enumerate(parts):
        side, k = n // 4, n % 4
        for xo in range(2):
            x_from = (x + xo) % 2
            at_p = side * 1024 + (xo * 4 + k) * 128
            at_s = pl.multiple_of(2048 + side * 1024 + (x_from * 4 + k) * 128, 128)
            c = (n * 2 + xo) * 4
            copies[side] += [
                pltpu.make_async_copy(ref.at[xo, 0:128, :], keys.at[at_p : at_p + 128, :], sem.at[c]),
                pltpu.make_async_copy(ref.at[xo, 256:512, 0:128], values_t.at[:, at_p : at_p + 128], sem.at[c + 1]),
            ]
            copies[2 + side] += [
                pltpu.make_async_copy(ref.at[xo, 128:256, :], keys.at[pl.ds(at_s, 128), :], sem.at[c + 2]),
                pltpu.make_async_copy(ref.at[xo, 256:512, 128:256], values_t.at[:, pl.ds(at_s, 128)], sem.at[c + 3]),
            ]
    for group in copies:
        for c in group:
            c.start()
    stack_queries(q, qs)
    m[...] = m_in[...]
    l[...] = l_in[...]
    acc[...] = acc_in[...]

    block_y = lax.rem(y - chunk + 4, 4)
    near_y = jnp.where(core == 1, y, 3 - y)
    far_y = 3 - near_y
    cut_core = jnp.where(near_y == block_y, core, 1 - core)
    row = lax.broadcasted_iota(jnp.int32, (1024, 128), 0)
    lane = lax.broadcasted_iota(jnp.int32, (1024, 128), 1)
    key_z = (z + 4 - (row // 128) % 4) % 4
    key_pos = 1024 * (row // 512) + 256 * key_z + 128 * cut_core + row % 128
    query_pos = 1024 * x + 256 * z + 128 * core + lane
    bias[0:1024, :] = jnp.zeros((1024, 128), F32)
    bias[1024:2048, :] = jnp.where(key_pos <= query_pos, 0.0, -jnp.inf)

    sees_near = near_y <= block_y
    sees_far = far_y <= block_y
    count = 2 + sees_near.astype(jnp.int32) + sees_far.astype(jnp.int32)

    def sweep(block, wait):
        def body(i, carry):
            at = jnp.where(jnp.logical_and(i == 2, jnp.logical_not(sees_near)), 3, i)
            if wait:
                for g in range(4):

                    @pl.when(i == g if g < 2 else jnp.logical_and(i == 2, g >= 2))
                    def _(g=g):
                        for c in copies[g]:
                            c.wait()

            from_y = jnp.where(at == 2, near_y, far_y)
            cut = jnp.logical_and(at >= 2, from_y == block_y)
            start = pl.multiple_of(at * 1024, 1024)
            b = bias[pl.ds(pl.multiple_of(jnp.where(cut, 1024, 0), 1024), 1024), :]
            for j in range(2):
                k = head_rows(keys, start, 1024, j)
                vt = values_t[j * 128 : (j + 1) * 128, pl.ds(start, 1024)]
                block(j, k, vt, qs, m, l, acc, b)
            return carry

        lax.fori_loop(0, count, body, 0)

    sweep(fast_block, True)

    @pl.when(count == 2)
    def _():
        for g in (2, 3):
            for c in copies[g]:
                c.wait()

    @pl.when(jnp.logical_not(is_safe(l, acc)))
    def _():
        m[...] = m_in[...]
        l[...] = l_in[...]
        acc[...] = acc_in[...]
        sweep(slow_block, False)

    for j in range(2):
        total = jnp.sum(l[j], axis=0, keepdims=True)
        out[j, 0:128, :] = (acc[j] * (1.0 / total)).astype(out.dtype)
        lse = jnp.broadcast_to(m[j, 0:1, :] + jnp.log(total) * math.log2(math.e), (16, 1024))
        if out.dtype == BF16:
            high = lse.astype(BF16).astype(F32)
            mid = (lse - high).astype(BF16).astype(F32)
            low = lse - high - mid
            place = lax.broadcasted_iota(jnp.int32, (16, 1024), 0)
            lse = jnp.where(place == 0, high, jnp.where(place == 1, mid, low))
        out[j, 128:144, :] = lse.astype(out.dtype)


def attend_fresh(info, chunk, q, state, parts):
    whole = pl.BlockSpec(memory_space=pltpu.VMEM)
    smem = pl.BlockSpec(memory_space=pltpu.SMEM)
    anywhere = pl.BlockSpec(memory_space=pl.ANY)
    return pl.pallas_call(
        functools.partial(fresh_kernel, chunk=chunk),
        grid=(1,),
        in_specs=[smem, whole]
        + [
            pl.BlockSpec((pl.squeezed, 2, 8, 1024), lambda i: (chunk, 0, 0, 0)),
            pl.BlockSpec((pl.squeezed, 2, 8, 1024), lambda i: (chunk, 0, 0, 0)),
            pl.BlockSpec((pl.squeezed, 2, 128, 1024), lambda i: (chunk, 0, 0, 0)),
        ]
        + [anywhere] * 8,
        out_specs=whole,
        out_shape=jax.ShapeDtypeStruct((2, 144, 1024), F32 if chunk == 0 else BF16),
        scratch_shapes=[
            pltpu.VMEM((4096, 256), BF16),
            pltpu.VMEM((256, 4096), BF16),
            pltpu.VMEM((2, 1024, 128), BF16),
            pltpu.VMEM((2048, 128), F32),
            pltpu.VMEM((2, 8, 1024), F32),
            pltpu.VMEM((2, 8, 1024), F32),
            pltpu.VMEM((2, 128, 1024), F32),
            pltpu.SemaphoreType.DMA((64,)),
        ],
        compiler_params=pltpu.CompilerParams(vmem_limit_bytes=VMEM_LIMIT),
        cost_estimate=pl.CostEstimate(flops=4 * 2048 * 3500 * 128, bytes_accessed=8 * 2**20, transcendentals=2048 * 3500),
        name=f"attend_fresh_{chunk}",
    )(info, q, *state, *parts)


def merge_kernel(own, one, two, three, out):
    parts = (own, one, two, three)
    for j in range(2):
        sizes = [own[j, 128:129, :]]
        for ref in parts[1:]:
            tail = ref[j, 128:144, :].astype(F32)
            sizes.append(tail[0:1] + tail[1:2] + tail[2:3])
        top = functools.reduce(jnp.maximum, sizes)
        shares = [jnp.exp2(size - top) for size in sizes]
        inverse = 1.0 / functools.reduce(jnp.add, shares)
        mixed = functools.reduce(
            jnp.add, [ref[j, 0:128, :].astype(F32) * (share * inverse) for ref, share in zip(parts, shares)]
        )
        for g in range(8):
            h = j * 8 + g
            out[:, h * 128 : (h + 1) * 128] = jnp.transpose(mixed[:, g * 128 : (g + 1) * 128]).astype(BF16)


def merge(parts):
    return pl.pallas_call(
        merge_kernel,
        in_specs=[pl.BlockSpec(memory_space=pltpu.VMEM)] * 4,
        out_specs=pl.BlockSpec(memory_space=pltpu.VMEM),
        out_shape=jax.ShapeDtypeStruct((128, 2048), BF16),
        compiler_params=pltpu.CompilerParams(vmem_limit_bytes=VMEM_LIMIT),
        name="merge",
    )(*parts)


def along_y(array, k):
    pairs = [(2 * y + x, 2 * ((y + k) % 4) + x) for y in range(4) for x in range(2)]
    return lax.ppermute(array, "store", pairs)


def along_z(array, k):
    return lax.ppermute(array, "ctx", [(i, (i + 2 * k) % 8) for i in range(8)])


def swap_x(array):
    return lax.ppermute(array, "store", [(i, i ^ 1) for i in range(8)])


def swap_cores(array):
    return lax.ppermute(array, "ctx", [(i, i ^ 1) for i in range(8)])


def swap_heads(array):
    return lax.ppermute(array, "head", [(0, 1), (1, 0)])


def mirror(array, heads):
    pairs = []
    for y in range(4):
        for x in range(2):
            for c in range(8):
                for h in range(2):
                    start = ((2 * y + x) * 8 + c) * 2 + h
                    if c % 2 == 0:
                        pairs.append((start, ((2 * (3 - y) + x) * 8 + c) * 2 + (h ^ heads)))
                    elif heads:
                        pairs.append((start, start ^ 1))
    return lax.ppermute(array, ("store", "ctx", "head"), pairs)


def per_device(queries, suffix_hidden, prefix_hidden, kv_cache, counts, w_key, w_value):
    store, ctx, head = lax.axis_index("store"), lax.axis_index("ctx"), lax.axis_index("head")
    y, x, z, core = store // 2, store % 2, ctx // 2, ctx % 2
    info = jnp.stack([y, x, z, core, head]).astype(jnp.int32)

    own, own_suffix, other_prefix, other_suffix = project(info, prefix_hidden, suffix_hidden, w_key, w_value)
    prefix_in = swap_heads(other_prefix)
    suffix_in = mirror(other_suffix, 1)
    moved_in = mirror(own_suffix, 0)

    queries_late, cache_late, _ = lax.optimization_barrier((queries, kv_cache, other_prefix))
    chunk_queries = [queries] + [along_y(queries_late, k) for k in range(1, 4)]
    half = lax.dynamic_slice(cache_late, (2 * core, 0, 0, 0), (2,) + kv_cache.shape[1:])
    same = swap_x(half)
    swapped = swap_cores(same)

    payload = combine(info, own, prefix_in, suffix_in, moved_in)
    pair = jnp.concatenate([payload, swap_x(payload)], axis=0)
    near = [pair] + [along_z(pair, k) for k in range(1, 4)]
    far = [swap_cores(part) for part in near]

    state = attend_cached(info, counts, chunk_queries, kv_cache, same, swapped)
    returned = {}
    for k in (2, 1, 3):
        returned[k] = along_y(attend_fresh(info, k, chunk_queries[k], state, near + far), -k)
    mine = attend_fresh(info, 0, queries, state, near + far)
    return merge([mine, returned[1], returned[2], returned[3]])


def solution(mesh):
    return jax.shard_map(
        per_device,
        mesh=mesh,
        in_specs=(
            P(("store", "ctx"), "head"),
            P(("store", "ctx"), "head"),
            P(("store", "ctx"), "head"),
            P("store", None, None, "head"),
            P(),
            P("head", None),
            P("head", None),
        ),
        out_specs=P(("store", "ctx"), "head"),
        check_vma=False,
    )
```

```python
import functools
import math

import jax
import jax.numpy as jnp
from jax import lax
from jax.experimental import pallas as pl
from jax.experimental.pallas import tpu as pltpu
from jax.sharding import PartitionSpec as P

HD = 128
SCALE = math.log2(math.e) / math.sqrt(HD)
SAFE = 2.0**100
F32 = jnp.float32
BF16 = jnp.bfloat16
VMEM_LIMIT = 56 * 2**20


def place():
    store, ctx = lax.axis_index("store"), lax.axis_index("ctx")
    return store // 2, store % 2, ctx // 2, ctx % 2


def project_kernel(xp, xs, wk, wv, own, other, acc_k, acc_v, *, steps, half):
    step = pl.program_id(0)
    head = lax.axis_index("head")

    @pl.when(step == 0)
    def _():
        acc_k[...] = jnp.zeros_like(acc_k)
        acc_v[...] = jnp.zeros_like(acc_v)

    x = jnp.concatenate([xp[...], xs[...]], axis=0)
    acc_k[...] += jnp.dot(x, wk[...], preferred_element_type=F32)
    acc_v[...] += jnp.dot(x, wv[...], preferred_element_type=F32)

    @pl.when(step == steps - 1)
    def _():
        mine = pl.ds(pl.multiple_of(head * half, half), half)
        theirs = pl.ds(pl.multiple_of((1 - head) * half, half), half)
        own[:, :half] = acc_k[:, mine]
        own[:, half:] = acc_v[:, mine]
        other[:, :half] = acc_k[:, theirs].astype(BF16)
        other[:, half:] = acc_v[:, theirs].astype(BF16)


def project(prefix, suffix, w_key, w_value):
    rows, feats = prefix.shape
    cols = w_key.shape[1]
    depth = 1024
    steps = feats // depth
    return pl.pallas_call(
        functools.partial(project_kernel, steps=steps, half=cols // 2),
        grid=(steps,),
        in_specs=[
            pl.BlockSpec((rows, depth), lambda i: (0, i)),
            pl.BlockSpec((rows, depth), lambda i: (0, i)),
            pl.BlockSpec((depth, cols), lambda i: (i, 0)),
            pl.BlockSpec((depth, cols), lambda i: (i, 0)),
        ],
        out_specs=[pl.BlockSpec((2 * rows, cols), lambda i: (0, 0))] * 2,
        out_shape=[jax.ShapeDtypeStruct((2 * rows, cols), F32), jax.ShapeDtypeStruct((2 * rows, cols), BF16)],
        scratch_shapes=[pltpu.VMEM((2 * rows, cols), F32), pltpu.VMEM((2 * rows, cols), F32)],
        compiler_params=pltpu.CompilerParams(vmem_limit_bytes=VMEM_LIMIT),
        cost_estimate=pl.CostEstimate(flops=1000, bytes_accessed=1000, transcendentals=0),
        name="project",
    )(prefix, suffix, w_key, w_value)


def combine_kernel(own, received, payload):
    rows, cols = own.shape
    half = cols // 2
    whole = (own[...] + received[...].astype(F32)).astype(BF16)
    payload[:rows, :] = whole[:, :half]
    payload[rows:, :] = jnp.transpose(whole[:, half:])


def combine(own, received):
    rows, cols = own.shape
    return pl.pallas_call(
        combine_kernel,
        in_specs=[pl.BlockSpec(memory_space=pltpu.VMEM)] * 2,
        out_specs=pl.BlockSpec(memory_space=pltpu.VMEM),
        out_shape=jax.ShapeDtypeStruct((rows + cols // 2, cols // 2), BF16),
        name="combine",
    )(own, received)


def stack_queries(q, qs):
    for j in range(2):
        for g in range(8):
            h = j * 8 + g
            qs[j, g * 128 : (g + 1) * 128, :] = q[:, h * 128 : (h + 1) * 128]


def scores_of(k, q):
    return lax.dot_general(k, q, (((1,), (1,)), ((), ())), preferred_element_type=F32)


def fast_block(j, k, vt, qs, m, l, acc, bias=None):
    size = k.shape[0]
    s = scores_of(k, qs[j])
    t = s.reshape(size // 8, 8, 1024) * SCALE - m[j][None]
    if bias is not None:
        t = t + jnp.concatenate([bias] * 8, axis=1).reshape(size // 8, 8, 1024)
    p = jnp.exp2(t)
    l[j] += jnp.sum(p, axis=0)
    acc[j] += jnp.dot(vt, p.reshape(size, 1024).astype(BF16), preferred_element_type=F32)


def slow_block(j, k, vt, qs, m, l, acc, bias=None):
    size = k.shape[0]
    s = scores_of(k, qs[j]) * SCALE
    if bias is not None:
        s = s + jnp.concatenate([bias] * 8, axis=1)
    old = m[j]
    top = jnp.broadcast_to(jnp.max(s, axis=0, keepdims=True), (8, 1024))
    new = jnp.maximum(old, top)
    m[j] = new
    shrink = jnp.exp2(old - new)
    p = jnp.exp2(s.reshape(size // 8, 8, 1024) - new[None])
    l[j] = l[j] * shrink + jnp.sum(p, axis=0)
    wide = jnp.broadcast_to(shrink[None], (16, 8, 1024)).reshape(128, 1024)
    acc[j] = acc[j] * wide + jnp.dot(vt, p.reshape(size, 1024).astype(BF16), preferred_element_type=F32)


def is_safe(l, acc):
    top = jnp.max(l[...])
    big = jnp.max(jnp.abs(acc[...]))
    return jnp.logical_and(top < SAFE, big < 1e36)


def head_rows(ref, start, size, j):
    return ref[pl.ds(start, size), j * 128 : (j + 1) * 128]


def cached_kernel(counts, *rest, slot_rows, chunks):
    queries = rest[:chunks]
    mine, same, swapped, m_out, l_out, acc_out, keys, values, values_t, qs, bias, sem = rest[chunks:]
    step = pl.program_id(0)
    y, x, _, core = place()
    owner, partner = 2 * y + x, 2 * y + 1 - x
    live = counts[owner] + counts[partner]

    @pl.when(step == 0)
    def _():
        slots = []
        sources = [(mine.at[t], t < counts[owner]) for t in range(4)]
        sources += [(same.at[t], 2 * core + t < counts[partner]) for t in range(2)]
        sources += [(swapped.at[t], 2 * (1 - core) + t < counts[partner]) for t in range(2)]
        at = jnp.int32(0)
        for n, (source, here) in enumerate(sources):
            rows = pl.ds(pl.multiple_of(at * slot_rows, slot_rows), slot_rows)
            slots.append(
                (
                    here,
                    rows,
                    pltpu.make_async_copy(source.at[0], keys.at[rows, :], sem.at[2 * n]),
                    pltpu.make_async_copy(source.at[1], values.at[rows, :], sem.at[2 * n + 1]),
                )
            )
            at = at + here.astype(jnp.int32)

        def at_live(act):
            for slot in slots:

                @pl.when(slot[0])
                def _(slot=slot):
                    act(*slot[1:])

        def start(rows, key_copy, value_copy):
            key_copy.start()
            value_copy.start()

        def finish(rows, key_copy, value_copy):
            key_copy.wait()
            value_copy.wait()
            values_t[:, rows] = jnp.transpose(values[rows, :])

        at_live(start)
        rest_rows = pl.ds(pl.multiple_of(jnp.minimum(live, 7) * slot_rows, slot_rows), slot_rows)

        @pl.when(live < 8)
        def _():
            keys[rest_rows, :] = jnp.zeros((slot_rows, keys.shape[1]), BF16)
            values_t[:, rest_rows] = jnp.zeros((keys.shape[1], slot_rows), BF16)

        at_live(finish)

    for i, q in enumerate(queries):

        @pl.when(step == i)
        def _(q=q):
            stack_queries(q, qs)

    m, l, acc = m_out, l_out, acc_out
    used = live * slot_rows
    blocks = (used + 511) // 512
    last = blocks - 1
    row = lax.broadcasted_iota(jnp.int32, (512, 128), 0)
    bias[...] = jnp.where(row + last * 512 < used, 0.0, -jnp.inf)

    for j in range(2):
        s = scores_of(keys[0:256, j * 128 : (j + 1) * 128], qs[j])
        m[j] = jnp.broadcast_to(jnp.max(s, axis=0, keepdims=True), (8, 1024)) * SCALE
    l[...] = jnp.zeros(l.shape, F32)
    acc[...] = jnp.zeros(acc.shape, F32)

    def sweep(block):
        def at(i, b):
            start = pl.multiple_of(i * 512, 512)
            for j in range(2):
                k = head_rows(keys, start, 512, j)
                vt = values_t[j * 128 : (j + 1) * 128, pl.ds(start, 512)]
                block(j, k, vt, qs, m, l, acc, b)

        def body(i, carry):
            at(i, None)
            return carry

        lax.fori_loop(0, last, body, 0)
        at(last, bias[...])

    sweep(fast_block)

    @pl.when(jnp.logical_not(is_safe(l, acc)))
    def _():
        l[...] = jnp.zeros(l.shape, F32)
        acc[...] = jnp.zeros(acc.shape, F32)
        sweep(slow_block)


def state_specs():
    return [
        pl.BlockSpec((pl.squeezed, 2, 8, 1024), lambda i: (i, 0, 0, 0)),
        pl.BlockSpec((pl.squeezed, 2, 8, 1024), lambda i: (i, 0, 0, 0)),
        pl.BlockSpec((pl.squeezed, 2, 128, 1024), lambda i: (i, 0, 0, 0)),
    ]


def attend_cached(counts, queries, cache, name):
    slot_rows = cache[0].shape[2]
    total = 8 * slot_rows
    rows = queries[0].shape[0]
    chunks = len(queries)
    whole = pl.BlockSpec(memory_space=pltpu.VMEM)
    smem = pl.BlockSpec(memory_space=pltpu.SMEM)
    return pl.pallas_call(
        functools.partial(cached_kernel, slot_rows=slot_rows, chunks=chunks),
        grid=(chunks,),
        in_specs=[smem] + [whole] * chunks + [pl.BlockSpec(memory_space=pl.ANY)] * 3,
        out_specs=state_specs(),
        out_shape=[
            jax.ShapeDtypeStruct((chunks, 2, 8, 1024), F32),
            jax.ShapeDtypeStruct((chunks, 2, 8, 1024), F32),
            jax.ShapeDtypeStruct((chunks, 2, 128, 1024), F32),
        ],
        scratch_shapes=[
            pltpu.VMEM((total, 256), BF16),
            pltpu.VMEM((total, 256), BF16),
            pltpu.VMEM((256, total), BF16),
            pltpu.VMEM((2, 1024, 128), BF16),
            pltpu.VMEM((512, 128), F32),
            pltpu.SemaphoreType.DMA((16,)),
        ],
        compiler_params=pltpu.CompilerParams(vmem_limit_bytes=VMEM_LIMIT),
        cost_estimate=pl.CostEstimate(flops=1000, bytes_accessed=1000, transcendentals=0),
        name=name,
    )(counts, *queries, *cache)


def fresh_kernel(*rest, chunks):
    queries, rest = rest[: len(chunks)], rest[len(chunks) :]
    states, rest = rest[: 3 * len(chunks)], rest[3 * len(chunks) :]
    parts, rest = rest[:10], rest[10:]
    outs, rest = rest[: len(chunks)], rest[len(chunks) :]
    keys, values_t, qs, bias, m, l, acc, sem = rest
    step = pl.program_id(0)
    first = step == 0
    chunk = jnp.int32(chunks[0])
    for i in range(1, len(chunks)):
        chunk = jnp.where(step == i, chunks[i], chunk)
    y, x, z, core = place()
    copies = [[], [], [], []]
    for n in range(8):
        side, k = n // 4, n % 4
        for xo in range(2):
            stacked, z2, x1, x2, x3 = parts[side * 5 : side * 5 + 5]
            ref = (stacked.at[0], stacked.at[1], stacked.at[2], x1, z2, x2, stacked.at[3], x3)[k * 2 + xo]
            x_from = (x + xo) % 2
            at_p = side * 1024 + (xo * 4 + k) * 128
            at_s = pl.multiple_of(2048 + side * 1024 + (x_from * 4 + k) * 128, 128)
            c = (n * 2 + xo) * 4
            copies[side] += [
                pltpu.make_async_copy(ref.at[0:128, :], keys.at[at_p : at_p + 128, :], sem.at[c]),
                pltpu.make_async_copy(ref.at[256:512, 0:128], values_t.at[:, at_p : at_p + 128], sem.at[c + 1]),
            ]
            copies[2 + side] += [
                pltpu.make_async_copy(ref.at[128:256, :], keys.at[pl.ds(at_s, 128), :], sem.at[c + 2]),
                pltpu.make_async_copy(ref.at[256:512, 128:256], values_t.at[:, pl.ds(at_s, 128)], sem.at[c + 3]),
            ]
    @pl.when(first)
    def _():
        for group in copies:
            for c in group:
                c.start()

    for i, q in enumerate(queries):

        @pl.when(step == i)
        def _(q=q):
            stack_queries(q, qs)

    def load_state():
        for i in range(len(chunks)):

            @pl.when(step == i)
            def _(i=i):
                for ref, source in zip((m, l, acc), states[3 * i : 3 * i + 3]):
                    ref[...] = source[0]

    load_state()
    block_y = lax.rem(y - chunk + 4, 4)
    row = lax.broadcasted_iota(jnp.int32, (2048, 128), 0)
    lane = lax.broadcasted_iota(jnp.int32, (2048, 128), 1)
    key_core = jnp.where(row < 1024, core, 1 - core)
    key_z = (z + 4 - (row // 128) % 4) % 4
    key_pos = 1024 * ((row // 512) % 2) + 256 * key_z + 128 * key_core + row % 128
    query_pos = 1024 * x + 256 * z + 128 * core + lane
    hidden = jnp.logical_and(y == block_y, key_pos > query_pos)
    bias[0:1024, :] = jnp.zeros((1024, 128), F32)
    bias[1024:3072, :] = jnp.where(hidden, -jnp.inf, 0.0)
    count = jnp.where(y <= block_y, 4, 2)

    def sweep(block, wait):
        def body(i, carry):
            if wait:
                for g in range(4):

                    @pl.when(jnp.logical_and(first, i == g))
                    def _(g=g):
                        for c in copies[g]:
                            c.wait()

            start = pl.multiple_of(i * 1024, 1024)
            b = bias[pl.ds(pl.multiple_of(jnp.maximum(i - 1, 0) * 1024, 1024), 1024), :]
            for j in range(2):
                k = head_rows(keys, start, 1024, j)
                vt = values_t[j * 128 : (j + 1) * 128, pl.ds(start, 1024)]
                block(j, k, vt, qs, m, l, acc, b)
            return carry

        lax.fori_loop(0, count, body, 0)

    sweep(fast_block, True)

    @pl.when(jnp.logical_and(first, count == 2))
    def _():
        for g in (2, 3):
            for c in copies[g]:
                c.wait()

    @pl.when(jnp.logical_not(is_safe(l, acc)))
    def _():
        load_state()
        sweep(slow_block, False)

    for i, out in enumerate(outs):

        @pl.when(step == i)
        def _(out=out):
            for j in range(2):
                total = jnp.sum(l[j], axis=0, keepdims=True)
                out[j, 0:128, :] = (acc[j] * (1.0 / total)).astype(out.dtype)
                lse = jnp.broadcast_to(m[j, 0:1, :] + jnp.log(total) * math.log2(math.e), (16, 1024))
                if out.dtype == BF16:
                    high = lse.astype(BF16).astype(F32)
                    mid = (lse - high).astype(BF16).astype(F32)
                    low = lse - high - mid
                    line = lax.broadcasted_iota(jnp.int32, (16, 1024), 0)
                    lse = jnp.where(line == 0, high, jnp.where(line == 1, mid, low))
                out[j, 128:144, :] = lse.astype(out.dtype)


def state_at(i):
    return [
        pl.BlockSpec((1, 2, 8, 1024), lambda _: (i, 0, 0, 0)),
        pl.BlockSpec((1, 2, 8, 1024), lambda _: (i, 0, 0, 0)),
        pl.BlockSpec((1, 2, 128, 1024), lambda _: (i, 0, 0, 0)),
    ]


def attend_fresh(chunks, queries, states, parts, dtype):
    whole = pl.BlockSpec(memory_space=pltpu.VMEM)
    anywhere = pl.BlockSpec(memory_space=pl.ANY)
    n = len(chunks)
    return pl.pallas_call(
        functools.partial(fresh_kernel, chunks=chunks),
        grid=(n,),
        in_specs=[whole] * n + [spec for _, i in states for spec in state_at(i)] + [anywhere] * 10,
        out_specs=[whole] * n,
        out_shape=[jax.ShapeDtypeStruct((2, 144, 1024), dtype)] * n,
        scratch_shapes=[
            pltpu.VMEM((4096, 256), BF16),
            pltpu.VMEM((256, 4096), BF16),
            pltpu.VMEM((2, 1024, 128), BF16),
            pltpu.VMEM((3072, 128), F32),
            pltpu.VMEM((2, 8, 1024), F32),
            pltpu.VMEM((2, 8, 1024), F32),
            pltpu.VMEM((2, 128, 1024), F32),
            pltpu.SemaphoreType.DMA((64,)),
        ],
        compiler_params=pltpu.CompilerParams(vmem_limit_bytes=VMEM_LIMIT),
        cost_estimate=pl.CostEstimate(flops=1000, bytes_accessed=1000, transcendentals=0),
        name="attend_fresh_" + "".join(str(c) for c in chunks),
    )(*queries, *[array for state, _ in states for array in state], *parts)


def merge_kernel(own, one, two, three, out):
    parts = (own, one, two, three)
    sizes = [own[128:129, :]]
    for ref in parts[1:]:
        tail = ref[128:144, :].astype(F32)
        sizes.append(tail[0:1] + tail[1:2] + tail[2:3])
    top = functools.reduce(jnp.maximum, sizes)
    shares = [jnp.exp2(size - top) for size in sizes]
    inverse = 1.0 / functools.reduce(jnp.add, shares)
    mixed = functools.reduce(
        jnp.add, [ref[0:128, :].astype(F32) * (share * inverse) for ref, share in zip(parts, shares)]
    )
    for g in range(mixed.shape[1] // 128):
        out[:, g * 128 : (g + 1) * 128] = jnp.transpose(mixed[:, g * 128 : (g + 1) * 128]).astype(BF16)


def merge(parts):
    width = 512
    return pl.pallas_call(
        merge_kernel,
        grid=(2048 // width,),
        in_specs=[pl.BlockSpec((pl.squeezed, 144, width), lambda i: (i // 2, 0, i % 2))] * 4,
        out_specs=pl.BlockSpec((128, width), lambda i: (0, i)),
        out_shape=jax.ShapeDtypeStruct((128, 2048), BF16),
        compiler_params=pltpu.CompilerParams(vmem_limit_bytes=VMEM_LIMIT),
        cost_estimate=pl.CostEstimate(flops=1000, bytes_accessed=1000, transcendentals=0),
        name="merge",
    )(*parts)


def along_y(array, k):
    pairs = [(2 * y + x, 2 * ((y + k) % 4) + x) for y in range(4) for x in range(2)]
    return lax.ppermute(array, "store", pairs)


def along_z(array, k):
    return lax.ppermute(array, "ctx", [(i, (i + 2 * k) % 8) for i in range(8)])


def swap_x(array):
    return lax.ppermute(array, "store", [(i, i ^ 1) for i in range(8)])


def swap_cores(array):
    return lax.ppermute(array, "ctx", [(i, i ^ 1) for i in range(8)])


def swap_heads(array):
    return lax.ppermute(array, "head", [(0, 1), (1, 0)])


def after(arrays, *others):
    return lax.optimization_barrier((tuple(arrays), others))[0]


def per_device(queries, suffix_hidden, prefix_hidden, kv_cache, counts, w_key, w_value):
    core = lax.axis_index("ctx") % 2
    half = lax.dynamic_slice(kv_cache, (2 * core, 0, 0, 0), (2,) + kv_cache.shape[1:])
    same = swap_x(half)
    q1 = along_y(queries, 1)

    own, other = project(prefix_hidden, suffix_hidden, w_key, w_value)
    received = swap_heads(other)
    token = other[:16, :128] * 2
    (late,) = after([queries], token)
    q2, q3 = along_y(late, 2), along_y(late, 3)
    (same,) = after([same], token)
    swapped = swap_cores(same)
    received, q1, q3, swapped = lax.optimization_barrier((received, q1, q3, swapped))
    payload = combine(own, received)

    by_x = swap_x(payload)
    z1, z3, z2 = along_z(payload, 1), along_z(payload, 3), along_z(payload, 2)
    cache = (kv_cache, same, swapped)
    (q0,) = after([queries], payload)
    state_01 = attend_cached(counts, [q0, q1], cache, "cached_01")

    by_x, z1, z2, z3, q2, q3 = after([by_x, z1, z2, z3, q2, q3], *state_01)
    x1, x3, x2 = along_z(by_x, 1), along_z(by_x, 3), along_z(by_x, 2)
    near_a = jnp.stack([payload, by_x, z1, z3])
    far_a, far_z2 = swap_cores(near_a), swap_cores(z2)
    q2, q3 = after([q2, q3], near_a)
    state_23 = attend_cached(counts, [q2, q3], cache, "cached_23")
    x1, x2, x3 = after([x1, x2, x3], *state_23)
    parts = [near_a, z2, x1, x2, x3, far_a, far_z2] + [swap_cores(part) for part in (x1, x2, x3)]

    (part_2,) = attend_fresh((2,), [q2], [(state_23, 0)], parts, BF16)
    two = along_y(part_2, -2)
    q1, q3 = after([q1, q3], part_2)
    part_1, part_3 = attend_fresh((1, 3), [q1, q3], [(state_01, 1), (state_23, 1)], parts, BF16)
    back_1, back_3 = along_y(part_1, -1), along_y(part_3, -3)
    (q0,) = after([queries], part_1, two)
    (mine,) = attend_fresh((0,), [q0], [(state_01, 0)], parts, F32)
    return merge([mine, back_1, two, back_3])


def solution(mesh):
    return jax.shard_map(
        per_device,
        mesh=mesh,
        in_specs=(
            P(("store", "ctx"), "head"),
            P(("store", "ctx"), "head"),
            P(("store", "ctx"), "head"),
            P("store", None, None, "head"),
            P(),
            P("head", None),
            P("head", None),
        ),
        out_specs=P(("store", "ctx"), "head"),
        check_vma=False,
    )
```

```python
import functools
import math

import jax
import jax.numpy as jnp
from jax import lax
from jax.experimental import pallas as pl
from jax.experimental.pallas import tpu as pltpu
from jax.sharding import PartitionSpec as P

HD = 128
SCALE = math.log2(math.e) / math.sqrt(HD)
SAFE = 2.0**100
F32 = jnp.float32
BF16 = jnp.bfloat16
VMEM_LIMIT = 64 * 2**20 - 2**17
ROOMY_LIMIT = 56 * 2**20


def place():
    store, ctx = lax.axis_index("store"), lax.axis_index("ctx")
    return store // 2, store % 2, ctx // 2, ctx % 2


def project_kernel(xp, xs, wk, wv, own, other, acc_k, acc_v, *, steps, half):
    step = pl.program_id(0)
    head = lax.axis_index("head")

    @pl.when(step == 0)
    def _():
        acc_k[...] = jnp.zeros_like(acc_k)
        acc_v[...] = jnp.zeros_like(acc_v)

    x = jnp.concatenate([xp[...], xs[...]], axis=0)
    acc_k[...] += jnp.dot(x, wk[...], preferred_element_type=F32)
    acc_v[...] += jnp.dot(x, wv[...], preferred_element_type=F32)

    @pl.when(step == steps - 1)
    def _():
        mine = pl.ds(pl.multiple_of(head * half, half), half)
        theirs = pl.ds(pl.multiple_of((1 - head) * half, half), half)
        own[:, :half] = acc_k[:, mine]
        own[:, half:] = acc_v[:, mine]
        other[:, :half] = acc_k[:, theirs].astype(BF16)
        other[:, half:] = acc_v[:, theirs].astype(BF16)


def project(prefix, suffix, w_key, w_value):
    rows, feats = prefix.shape
    cols = w_key.shape[1]
    depth = 1024
    steps = feats // depth
    return pl.pallas_call(
        functools.partial(project_kernel, steps=steps, half=cols // 2),
        grid=(steps,),
        in_specs=[
            pl.BlockSpec((rows, depth), lambda i: (0, i)),
            pl.BlockSpec((rows, depth), lambda i: (0, i)),
            pl.BlockSpec((depth, cols), lambda i: (i, 0)),
            pl.BlockSpec((depth, cols), lambda i: (i, 0)),
        ],
        out_specs=[pl.BlockSpec((2 * rows, cols), lambda i: (0, 0))] * 2,
        out_shape=[jax.ShapeDtypeStruct((2 * rows, cols), F32), jax.ShapeDtypeStruct((2 * rows, cols), BF16)],
        scratch_shapes=[pltpu.VMEM((2 * rows, cols), F32), pltpu.VMEM((2 * rows, cols), F32)],
        compiler_params=pltpu.CompilerParams(vmem_limit_bytes=ROOMY_LIMIT),
        cost_estimate=pl.CostEstimate(flops=1000, bytes_accessed=1000, transcendentals=0),
        name="project",
    )(prefix, suffix, w_key, w_value)


def combine_kernel(own_hbm, received_hbm, payload, own, received, sem):
    rows, cols = own.shape
    half = cols // 2
    keys, values = pl.ds(0, half), pl.ds(half, half)
    copies = []
    for i, part in enumerate((values, keys)):
        copies.append(
            (
                pltpu.make_async_copy(own_hbm.at[:, part], own.at[:, part], sem.at[2 * i]),
                pltpu.make_async_copy(received_hbm.at[:, part], received.at[:, part], sem.at[2 * i + 1]),
            )
        )
    for pair in copies:
        for c in pair:
            c.start()
    for c in copies[0]:
        c.wait()
    payload[rows:, :] = jnp.transpose((own[:, values] + received[:, values].astype(F32)).astype(BF16))
    for c in copies[1]:
        c.wait()
    payload[:rows, :] = (own[:, keys] + received[:, keys].astype(F32)).astype(BF16)


def combine(own, received):
    rows, cols = own.shape
    return pl.pallas_call(
        combine_kernel,
        in_specs=[pl.BlockSpec(memory_space=pl.ANY)] * 2,
        out_specs=pl.BlockSpec(memory_space=pltpu.VMEM),
        out_shape=jax.ShapeDtypeStruct((rows + cols // 2, cols // 2), BF16),
        scratch_shapes=[pltpu.VMEM((rows, cols), F32), pltpu.VMEM((rows, cols), BF16), pltpu.SemaphoreType.DMA((4,))],
        compiler_params=pltpu.CompilerParams(vmem_limit_bytes=VMEM_LIMIT),
        name="combine",
    )(own, received)


def stack_queries(q, qs):
    for j in range(2):
        for g in range(8):
            h = j * 8 + g
            qs[j, g * 128 : (g + 1) * 128, :] = q[:, h * 128 : (h + 1) * 128]


def scores_of(k, q):
    return lax.dot_general(k, q, (((1,), (1,)), ((), ())), preferred_element_type=F32)


def fast_block(j, k, vt, qs, m, l, acc, bias=None):
    size = k.shape[0]
    s = scores_of(k, qs[j])
    t = s.reshape(size // 8, 8, 1024) * SCALE - m[j][None]
    if bias is not None:
        t = t + jnp.concatenate([bias] * 8, axis=1).reshape(size // 8, 8, 1024)
    p = jnp.exp2(t)
    l[j] += jnp.sum(p, axis=0)
    acc[j] += jnp.dot(vt, p.reshape(size, 1024).astype(BF16), preferred_element_type=F32)


def slow_block(j, k, vt, qs, m, l, acc, bias=None):
    size = k.shape[0]
    s = scores_of(k, qs[j]) * SCALE
    if bias is not None:
        s = s + jnp.concatenate([bias] * 8, axis=1)
    old = m[j]
    top = jnp.broadcast_to(jnp.max(s, axis=0, keepdims=True), (8, 1024))
    new = jnp.maximum(old, top)
    m[j] = new
    shrink = jnp.exp2(old - new)
    p = jnp.exp2(s.reshape(size // 8, 8, 1024) - new[None])
    l[j] = l[j] * shrink + jnp.sum(p, axis=0)
    wide = jnp.broadcast_to(shrink[None], (16, 8, 1024)).reshape(128, 1024)
    acc[j] = acc[j] * wide + jnp.dot(vt, p.reshape(size, 1024).astype(BF16), preferred_element_type=F32)


def is_safe(l, acc):
    top = jnp.max(l[...])
    big = jnp.max(jnp.abs(acc[...]))
    return jnp.logical_and(top < SAFE, big < 1e36)


def head_rows(ref, start, size, j):
    return ref[pl.ds(start, size), j * 128 : (j + 1) * 128]


def cached_kernel(counts, *rest, slot_rows, chunks):
    queries = rest[:chunks]
    mine, same, swapped, m_out, l_out, acc_out, keys, values, values_t, q_all, qs, sem = rest[chunks:]
    step = pl.program_id(0)
    y, x, _, core = place()
    owner, partner = 2 * y + x, 2 * y + 1 - x
    live = counts[owner] + counts[partner]

    query_copies = [pltpu.make_async_copy(q, q_all.at[i], sem.at[16 + i]) for i, q in enumerate(queries)]

    @pl.when(step == 0)
    def _():
        slots = []
        sources = [(mine.at[t], t < counts[owner]) for t in range(4)]
        sources += [(same.at[t], 2 * core + t < counts[partner]) for t in range(2)]
        sources += [(swapped.at[t], 2 * (1 - core) + t < counts[partner]) for t in range(2)]
        at = jnp.int32(0)
        for n, (source, here) in enumerate(sources):
            rows = pl.ds(pl.multiple_of(at * slot_rows, slot_rows), slot_rows)
            slots.append(
                (
                    here,
                    rows,
                    pltpu.make_async_copy(source.at[0], keys.at[rows, :], sem.at[2 * n]),
                    pltpu.make_async_copy(source.at[1], values.at[rows, :], sem.at[2 * n + 1]),
                )
            )
            at = at + here.astype(jnp.int32)

        def at_live(act):
            for slot in slots:

                @pl.when(slot[0])
                def _(slot=slot):
                    act(*slot[1:])

        def start(rows, key_copy, value_copy):
            key_copy.start()
            value_copy.start()

        def finish(rows, key_copy, value_copy):
            key_copy.wait()
            value_copy.wait()
            values_t[:, rows] = jnp.transpose(values[rows, :])

        for copy in query_copies:
            copy.start()
        at_live(start)
        at_live(finish)

    for i, copy in enumerate(query_copies):

        @pl.when(step == i)
        def _(copy=copy):
            copy.wait()

    stack_queries(q_all.at[step], qs)

    m, l, acc = m_out, l_out, acc_out
    used = live * slot_rows

    for j in range(2):
        s = scores_of(keys[0:256, j * 128 : (j + 1) * 128], qs[j])
        m[j] = jnp.broadcast_to(jnp.max(s, axis=0, keepdims=True), (8, 1024)) * SCALE
    l[...] = jnp.zeros(l.shape, F32)
    acc[...] = jnp.zeros(acc.shape, F32)

    def sweep(block):
        def at(start, size):
            for j in range(2):
                k = head_rows(keys, start, size, j)
                vt = values_t[j * 128 : (j + 1) * 128, pl.ds(start, size)]
                block(j, k, vt, qs, m, l, acc)

        def body(i, carry):
            at(pl.multiple_of(i * 1024, 1024), 1024)
            return carry

        lax.fori_loop(0, used // 1024, body, 0)

        @pl.when(used % 1024 >= 512)
        def _():
            at(pl.multiple_of(used // 1024 * 1024, 1024), 512)

        @pl.when(used % 512 > 0)
        def _():
            at(pl.multiple_of(used // 512 * 512, 512), 256)

    sweep(fast_block)

    @pl.when(jnp.logical_not(is_safe(l, acc)))
    def _():
        l[...] = jnp.zeros(l.shape, F32)
        acc[...] = jnp.zeros(acc.shape, F32)
        sweep(slow_block)


def state_specs():
    return [
        pl.BlockSpec((pl.squeezed, 2, 8, 1024), lambda i: (i, 0, 0, 0)),
        pl.BlockSpec((pl.squeezed, 2, 8, 1024), lambda i: (i, 0, 0, 0)),
        pl.BlockSpec((pl.squeezed, 2, 128, 1024), lambda i: (i, 0, 0, 0)),
    ]


def attend_cached(counts, queries, cache, name):
    slot_rows = cache[0].shape[2]
    total = 8 * slot_rows
    rows = queries[0].shape[0]
    chunks = len(queries)
    smem = pl.BlockSpec(memory_space=pltpu.SMEM)
    return pl.pallas_call(
        functools.partial(cached_kernel, slot_rows=slot_rows, chunks=chunks),
        grid=(chunks,),
        in_specs=[smem] + [pl.BlockSpec(memory_space=pl.ANY)] * (chunks + 3),
        out_specs=state_specs(),
        out_shape=[
            jax.ShapeDtypeStruct((chunks, 2, 8, 1024), F32),
            jax.ShapeDtypeStruct((chunks, 2, 8, 1024), F32),
            jax.ShapeDtypeStruct((chunks, 2, 128, 1024), F32),
        ],
        scratch_shapes=[
            pltpu.VMEM((total, 256), BF16),
            pltpu.VMEM((total, 256), BF16),
            pltpu.VMEM((256, total), BF16),
            pltpu.VMEM((chunks, rows, 2048), BF16),
            pltpu.VMEM((2, 1024, 128), BF16),
            pltpu.SemaphoreType.DMA((16 + chunks,)),
        ],
        compiler_params=pltpu.CompilerParams(vmem_limit_bytes=ROOMY_LIMIT),
        cost_estimate=pl.CostEstimate(flops=1000, bytes_accessed=1000, transcendentals=0),
        name=name,
    )(counts, *queries, *cache)


def fresh_kernel(*rest, chunks):
    queries, rest = rest[: len(chunks)], rest[len(chunks) :]
    states, rest = rest[: 3 * len(chunks)], rest[3 * len(chunks) :]
    parts, rest = rest[:8], rest[8:]
    outs, rest = rest[: len(chunks)], rest[len(chunks) :]
    keys, values_t, q_all, qs, bias, m, l, acc, sem = rest
    step = pl.program_id(0)
    first = step == 0
    chunk = jnp.int32(chunks[0])
    for i in range(1, len(chunks)):
        chunk = jnp.where(step == i, chunks[i], chunk)
    y, x, z, core = place()
    copies = [[], [], [], []]
    for n in range(8):
        side, k = n // 4, n % 4
        for xo in range(2):
            stacked, x1, x3, two = parts[side * 4 : side * 4 + 4]
            ref = (stacked.at[0], stacked.at[1], stacked.at[2], x1, two.at[0], two.at[1], stacked.at[3], x3)[k * 2 + xo]
            x_from = (x + xo) % 2
            at_p = side * 1024 + (xo * 4 + k) * 128
            at_s = pl.multiple_of(2048 + side * 1024 + (x_from * 4 + k) * 128, 128)
            c = (n * 2 + xo) * 4
            copies[side] += [
                pltpu.make_async_copy(ref.at[0:128, :], keys.at[at_p : at_p + 128, :], sem.at[c]),
                pltpu.make_async_copy(ref.at[256:512, 0:128], values_t.at[:, at_p : at_p + 128], sem.at[c + 1]),
            ]
            copies[2 + side] += [
                pltpu.make_async_copy(ref.at[128:256, :], keys.at[pl.ds(at_s, 128), :], sem.at[c + 2]),
                pltpu.make_async_copy(ref.at[256:512, 128:256], values_t.at[:, pl.ds(at_s, 128)], sem.at[c + 3]),
            ]
    query_copies = [pltpu.make_async_copy(q, q_all.at[i], sem.at[64 + i]) for i, q in enumerate(queries)]

    @pl.when(first)
    def _():
        for group in [query_copies] + copies:
            for c in group:
                c.start()

    for i, copy in enumerate(query_copies):

        @pl.when(step == i)
        def _(copy=copy):
            copy.wait()

    stack_queries(q_all.at[step], qs)

    def load_state():
        for i in range(len(chunks)):

            @pl.when(step == i)
            def _(i=i):
                for ref, source in zip((m, l, acc), states[3 * i : 3 * i + 3]):
                    ref[...] = source[0]

    load_state()
    block_y = y ^ chunk
    row = lax.broadcasted_iota(jnp.int32, (2048, 128), 0)
    lane = lax.broadcasted_iota(jnp.int32, (2048, 128), 1)
    key_core = jnp.where(row < 1024, core, 1 - core)
    key_z = z ^ ((row // 128) % 4)
    key_pos = 1024 * ((row // 512) % 2) + 256 * key_z + 128 * key_core + row % 128
    query_pos = 1024 * x + 256 * z + 128 * core + lane
    hidden = jnp.logical_and(y == block_y, key_pos > query_pos)
    bias[0:1024, :] = jnp.zeros((1024, 128), F32)
    bias[1024:3072, :] = jnp.where(hidden, -jnp.inf, 0.0)
    count = jnp.where(y <= block_y, 4, 2)

    def sweep(block, wait):
        def body(i, carry):
            if wait:
                for g in range(4):

                    @pl.when(jnp.logical_and(first, i == g))
                    def _(g=g):
                        for c in copies[g]:
                            c.wait()

            start = pl.multiple_of(i * 1024, 1024)
            b = bias[pl.ds(pl.multiple_of(jnp.maximum(i - 1, 0) * 1024, 1024), 1024), :]
            for j in range(2):
                k = head_rows(keys, start, 1024, j)
                vt = values_t[j * 128 : (j + 1) * 128, pl.ds(start, 1024)]
                block(j, k, vt, qs, m, l, acc, b)
            return carry

        lax.fori_loop(0, count, body, 0)

    sweep(fast_block, True)

    @pl.when(jnp.logical_and(first, count == 2))
    def _():
        for g in (2, 3):
            for c in copies[g]:
                c.wait()

    @pl.when(jnp.logical_not(is_safe(l, acc)))
    def _():
        load_state()
        sweep(slow_block, False)

    for i, out in enumerate(outs):

        @pl.when(step == i)
        def _(out=out):
            for j in range(2):
                total = jnp.sum(l[j], axis=0, keepdims=True)
                out[j, 0:128, :] = (acc[j] * (1.0 / total)).astype(out.dtype)
                lse = jnp.broadcast_to(m[j, 0:1, :] + jnp.log(total) * math.log2(math.e), (16, 1024))
                if out.dtype == BF16:
                    high = lse.astype(BF16).astype(F32)
                    mid = (lse - high).astype(BF16).astype(F32)
                    low = lse - high - mid
                    line = lax.broadcasted_iota(jnp.int32, (16, 1024), 0)
                    lse = jnp.where(line == 0, high, jnp.where(line == 1, mid, low))
                out[j, 128:144, :] = lse.astype(out.dtype)


def state_at(i):
    return [
        pl.BlockSpec((1, 2, 8, 1024), lambda _: (i, 0, 0, 0)),
        pl.BlockSpec((1, 2, 8, 1024), lambda _: (i, 0, 0, 0)),
        pl.BlockSpec((1, 2, 128, 1024), lambda _: (i, 0, 0, 0)),
    ]


def attend_fresh(chunks, queries, states, parts, dtype):
    whole = pl.BlockSpec(memory_space=pltpu.VMEM)
    anywhere = pl.BlockSpec(memory_space=pl.ANY)
    n = len(chunks)
    return pl.pallas_call(
        functools.partial(fresh_kernel, chunks=chunks),
        grid=(n,),
        in_specs=[anywhere] * n + [spec for _, i in states for spec in state_at(i)] + [anywhere] * 8,
        out_specs=[whole] * n,
        out_shape=[jax.ShapeDtypeStruct((2, 144, 1024), dtype)] * n,
        scratch_shapes=[
            pltpu.VMEM((4096, 256), BF16),
            pltpu.VMEM((256, 4096), BF16),
            pltpu.VMEM((n, 128, 2048), BF16),
            pltpu.VMEM((2, 1024, 128), BF16),
            pltpu.VMEM((3072, 128), F32),
            pltpu.VMEM((2, 8, 1024), F32),
            pltpu.VMEM((2, 8, 1024), F32),
            pltpu.VMEM((2, 128, 1024), F32),
            pltpu.SemaphoreType.DMA((64 + n,)),
        ],
        compiler_params=pltpu.CompilerParams(vmem_limit_bytes=VMEM_LIMIT),
        cost_estimate=pl.CostEstimate(flops=1000, bytes_accessed=1000, transcendentals=0),
        name="attend_fresh_" + "".join(str(c) for c in chunks),
    )(*queries, *[array for state, _ in states for array in state], *parts)


def merge_kernel(own, one, two, three, out):
    parts = (own, one, two, three)
    sizes = [own[128:129, :]]
    for ref in parts[1:]:
        tail = ref[128:144, :].astype(F32)
        sizes.append(tail[0:1] + tail[1:2] + tail[2:3])
    top = functools.reduce(jnp.maximum, sizes)
    shares = [jnp.exp2(size - top) for size in sizes]
    inverse = 1.0 / functools.reduce(jnp.add, shares)
    mixed = functools.reduce(
        jnp.add, [ref[0:128, :].astype(F32) * (share * inverse) for ref, share in zip(parts, shares)]
    )
    mixed = mixed.astype(BF16)
    for g in range(mixed.shape[1] // 128):
        out[:, g * 128 : (g + 1) * 128] = jnp.transpose(mixed[:, g * 128 : (g + 1) * 128])


def merge(parts):
    width = 1024
    return pl.pallas_call(
        merge_kernel,
        grid=(2048 // width,),
        in_specs=[pl.BlockSpec((pl.squeezed, 144, width), lambda i: (i, 0, 0))] * 4,
        out_specs=pl.BlockSpec((128, width), lambda i: (0, i)),
        out_shape=jax.ShapeDtypeStruct((128, 2048), BF16),
        compiler_params=pltpu.CompilerParams(vmem_limit_bytes=VMEM_LIMIT),
        cost_estimate=pl.CostEstimate(flops=1000, bytes_accessed=1000, transcendentals=0),
        name="merge",
    )(*parts)


def along_y(array, k):
    pairs = [(2 * y + x, 2 * (y ^ k) + x) for y in range(4) for x in range(2)]
    return lax.ppermute(array, "store", pairs)


def along_z(array, k):
    return lax.ppermute(array, "ctx", [(i, i ^ (2 * k)) for i in range(8)])


def swap_x(array):
    return lax.ppermute(array, "store", [(i, i ^ 1) for i in range(8)])


def swap_cores(array):
    return lax.ppermute(array, "ctx", [(i, i ^ 1) for i in range(8)])


def swap_heads(array):
    return lax.ppermute(array, "head", [(0, 1), (1, 0)])


def after(arrays, *others):
    return lax.optimization_barrier((tuple(arrays), others))[0]


def per_device(queries, suffix_hidden, prefix_hidden, kv_cache, counts, w_key, w_value):
    core = lax.axis_index("ctx") % 2
    own, other = project(prefix_hidden, suffix_hidden, w_key, w_value)
    received = swap_heads(other)
    half = lax.dynamic_slice(kv_cache, (2 * core, 0, 0, 0), (2,) + kv_cache.shape[1:])
    same = swap_x(half)
    q1, q3 = along_y(queries, 1), along_y(queries, 3)
    received, q1, q3 = lax.optimization_barrier((received, q1, q3))
    payload = combine(own, received)

    late, same = after([queries, same], payload)
    by_x = swap_x(payload)
    z1, z3 = along_z(payload, 1), along_z(payload, 3)
    q2, swapped = along_y(late, 2), swap_cores(same)
    cache = (kv_cache, same, swapped)
    (q0,) = after([queries], payload)
    state_01 = attend_cached(counts, [q0, q1], cache, "cached_01")

    by_x, z1, z3, q2 = after([by_x, z1, z3, q2], *state_01)
    x1, x3 = along_z(by_x, 1), along_z(by_x, 3)
    near_a = jnp.stack([payload, by_x, z1, z3])
    two_z = along_z(near_a[0:2], 2)
    far_a = swap_cores(near_a)
    q2, q3 = after([q2, q3], near_a)
    state_23 = attend_cached(counts, [q2, q3], cache, "cached_23")
    tail = after([x1, x3, two_z], *state_23)
    parts = [near_a, *tail, far_a] + [swap_cores(part) for part in tail]

    (part_2,) = attend_fresh((2,), [q2], [(state_23, 0)], parts, BF16)
    two = along_y(part_2, 2)
    q1, q3 = after([q1, q3], part_2)
    part_1, part_3 = attend_fresh((1, 3), [q1, q3], [(state_01, 1), (state_23, 1)], parts, BF16)
    back_1, back_3 = along_y(part_1, 1), along_y(part_3, 3)
    (q0,) = after([queries], part_1, two)
    (mine,) = attend_fresh((0,), [q0], [(state_01, 0)], parts, F32)
    return merge([mine, back_1, two, back_3])


def solution(mesh):
    return jax.shard_map(
        per_device,
        mesh=mesh,
        in_specs=(
            P(("store", "ctx"), "head"),
            P(("store", "ctx"), "head"),
            P(("store", "ctx"), "head"),
            P("store", None, None, "head"),
            P(),
            P("head", None),
            P("head", None),
        ),
        out_specs=P(("store", "ctx"), "head"),
        check_vma=False,
    )
```

```python
import functools
import math

import jax
import jax.numpy as jnp
from jax import lax
from jax.experimental import pallas as pl
from jax.experimental.pallas import tpu as pltpu
from jax.sharding import PartitionSpec as P

HD = 128
SCALE = math.log2(math.e) / math.sqrt(HD)
SAFE = 2.0**100
F32 = jnp.float32
BF16 = jnp.bfloat16
VMEM_LIMIT = 64 * 2**20 - 2**17
ROOMY_LIMIT = 56 * 2**20


def place():
    store, ctx = lax.axis_index("store"), lax.axis_index("ctx")
    return store // 2, store % 2, ctx // 2, ctx % 2


def project_kernel(xp, xs, wk, wv, own, other, acc_k, acc_v, *, steps, half):
    step = pl.program_id(0)
    head = lax.axis_index("head")

    @pl.when(step == 0)
    def _():
        acc_k[...] = jnp.zeros_like(acc_k)
        acc_v[...] = jnp.zeros_like(acc_v)

    x = jnp.concatenate([xp[...], xs[...]], axis=0)
    acc_k[...] += jnp.dot(x, wk[...], preferred_element_type=F32)
    acc_v[...] += jnp.dot(x, wv[...], preferred_element_type=F32)

    @pl.when(step == steps - 1)
    def _():
        mine = pl.ds(pl.multiple_of(head * half, half), half)
        theirs = pl.ds(pl.multiple_of((1 - head) * half, half), half)
        own[:, :half] = acc_k[:, mine]
        own[:, half:] = acc_v[:, mine]
        other[:, :half] = acc_k[:, theirs].astype(BF16)
        other[:, half:] = acc_v[:, theirs].astype(BF16)


def project(prefix, suffix, w_key, w_value):
    rows, feats = prefix.shape
    cols = w_key.shape[1]
    depth = 2048
    steps = feats // depth
    return pl.pallas_call(
        functools.partial(project_kernel, steps=steps, half=cols // 2),
        grid=(steps,),
        in_specs=[
            pl.BlockSpec((rows, depth), lambda i: (0, i)),
            pl.BlockSpec((rows, depth), lambda i: (0, i)),
            pl.BlockSpec((depth, cols), lambda i: (i, 0)),
            pl.BlockSpec((depth, cols), lambda i: (i, 0)),
        ],
        out_specs=[pl.BlockSpec((2 * rows, cols), lambda i: (0, 0))] * 2,
        out_shape=[jax.ShapeDtypeStruct((2 * rows, cols), F32), jax.ShapeDtypeStruct((2 * rows, cols), BF16)],
        scratch_shapes=[pltpu.VMEM((2 * rows, cols), F32), pltpu.VMEM((2 * rows, cols), F32)],
        compiler_params=pltpu.CompilerParams(vmem_limit_bytes=ROOMY_LIMIT),
        cost_estimate=pl.CostEstimate(flops=1000, bytes_accessed=1000, transcendentals=0),
        name="project",
    )(prefix, suffix, w_key, w_value)


def combine_kernel(own_hbm, received_hbm, payload, own, received, sem):
    rows, cols = own.shape
    half = cols // 2
    keys, values = pl.ds(0, half), pl.ds(half, half)
    copies = []
    for i, part in enumerate((values, keys)):
        copies.append(
            (
                pltpu.make_async_copy(own_hbm.at[:, part], own.at[:, part], sem.at[2 * i]),
                pltpu.make_async_copy(received_hbm.at[:, part], received.at[:, part], sem.at[2 * i + 1]),
            )
        )
    for pair in copies:
        for c in pair:
            c.start()
    for c in copies[0]:
        c.wait()
    payload[rows:, :] = jnp.transpose((own[:, values] + received[:, values].astype(F32)).astype(BF16))
    for c in copies[1]:
        c.wait()
    payload[:rows, :] = (own[:, keys] + received[:, keys].astype(F32)).astype(BF16)


def combine(own, received):
    rows, cols = own.shape
    return pl.pallas_call(
        combine_kernel,
        in_specs=[pl.BlockSpec(memory_space=pl.ANY)] * 2,
        out_specs=pl.BlockSpec(memory_space=pltpu.VMEM),
        out_shape=jax.ShapeDtypeStruct((rows + cols // 2, cols // 2), BF16),
        scratch_shapes=[pltpu.VMEM((rows, cols), F32), pltpu.VMEM((rows, cols), BF16), pltpu.SemaphoreType.DMA((4,))],
        compiler_params=pltpu.CompilerParams(vmem_limit_bytes=VMEM_LIMIT),
        name="combine",
    )(own, received)


def stack_queries(q, qs):
    for j in range(2):
        for g in range(8):
            h = j * 8 + g
            qs[j, g * 128 : (g + 1) * 128, :] = q[:, h * 128 : (h + 1) * 128]


def scores_of(k, q):
    return lax.dot_general(k, q, (((1,), (1,)), ((), ())), preferred_element_type=F32)


def fast_block(j, k, vt, qs, m, l, acc, bias=None):
    size = k.shape[0]
    s = scores_of(k, qs[j])
    t = s.reshape(size // 8, 8, 1024) * SCALE - m[j][None]
    if bias is not None:
        t = t + jnp.concatenate([bias] * 8, axis=1).reshape(size // 8, 8, 1024)
    p = jnp.exp2(t)
    l[j] += jnp.sum(p, axis=0)
    acc[j] += jnp.dot(vt, p.reshape(size, 1024).astype(BF16), preferred_element_type=F32)


def slow_block(j, k, vt, qs, m, l, acc, bias=None):
    size = k.shape[0]
    s = scores_of(k, qs[j]) * SCALE
    if bias is not None:
        s = s + jnp.concatenate([bias] * 8, axis=1)
    old = m[j]
    top = jnp.broadcast_to(jnp.max(s, axis=0, keepdims=True), (8, 1024))
    new = jnp.maximum(old, top)
    m[j] = new
    shrink = jnp.exp2(old - new)
    p = jnp.exp2(s.reshape(size // 8, 8, 1024) - new[None])
    l[j] = l[j] * shrink + jnp.sum(p, axis=0)
    wide = jnp.broadcast_to(shrink[None], (16, 8, 1024)).reshape(128, 1024)
    acc[j] = acc[j] * wide + jnp.dot(vt, p.reshape(size, 1024).astype(BF16), preferred_element_type=F32)


def is_safe(l, acc):
    top = jnp.max(l[...])
    big = jnp.max(jnp.abs(acc[...]))
    return jnp.logical_and(top < SAFE, big < 1e36)


def head_rows(ref, start, size, j):
    return ref[pl.ds(start, size), j * 128 : (j + 1) * 128]


def cached_kernel(counts, *rest, slot_rows, chunks):
    queries = rest[:chunks]
    mine, same, swapped, m_out, l_out, acc_out, keys, values, values_t, q_all, qs, sem = rest[chunks:]
    step = pl.program_id(0)
    y, x, _, core = place()
    owner, partner = 2 * y + x, 2 * y + 1 - x
    live = counts[owner] + counts[partner]

    query_copies = [pltpu.make_async_copy(q, q_all.at[i], sem.at[16 + i]) for i, q in enumerate(queries)]

    @pl.when(step == 0)
    def _():
        slots = []
        sources = [(mine.at[t], t < counts[owner]) for t in range(4)]
        sources += [(same.at[t], 2 * core + t < counts[partner]) for t in range(2)]
        sources += [(swapped.at[t], 2 * (1 - core) + t < counts[partner]) for t in range(2)]
        at = jnp.int32(0)
        for n, (source, here) in enumerate(sources):
            rows = pl.ds(pl.multiple_of(at * slot_rows, slot_rows), slot_rows)
            slots.append(
                (
                    here,
                    rows,
                    pltpu.make_async_copy(source.at[0], keys.at[rows, :], sem.at[2 * n]),
                    pltpu.make_async_copy(source.at[1], values.at[rows, :], sem.at[2 * n + 1]),
                )
            )
            at = at + here.astype(jnp.int32)

        def at_live(act):
            for slot in slots:

                @pl.when(slot[0])
                def _(slot=slot):
                    act(*slot[1:])

        def start(rows, key_copy, value_copy):
            key_copy.start()
            value_copy.start()

        def finish(rows, key_copy, value_copy):
            key_copy.wait()
            value_copy.wait()
            values_t[:, rows] = jnp.transpose(values[rows, :])

        for copy in query_copies:
            copy.start()
        at_live(start)
        at_live(finish)

    for i, copy in enumerate(query_copies):

        @pl.when(step == i)
        def _(copy=copy):
            copy.wait()

    stack_queries(q_all.at[step], qs)

    m, l, acc = m_out, l_out, acc_out
    used = live * slot_rows

    for j in range(2):
        s = scores_of(keys[0:256, j * 128 : (j + 1) * 128], qs[j])
        m[j] = jnp.broadcast_to(jnp.max(s, axis=0, keepdims=True), (8, 1024)) * SCALE
    l[...] = jnp.zeros(l.shape, F32)
    acc[...] = jnp.zeros(acc.shape, F32)

    def sweep(block):
        def at(start, size):
            for j in range(2):
                k = head_rows(keys, start, size, j)
                vt = values_t[j * 128 : (j + 1) * 128, pl.ds(start, size)]
                block(j, k, vt, qs, m, l, acc)

        def body(i, carry):
            at(pl.multiple_of(i * 1024, 1024), 1024)
            return carry

        lax.fori_loop(0, used // 1024, body, 0)

        @pl.when(used % 1024 >= 512)
        def _():
            at(pl.multiple_of(used // 1024 * 1024, 1024), 512)

        @pl.when(used % 512 > 0)
        def _():
            at(pl.multiple_of(used // 512 * 512, 512), 256)

    sweep(fast_block)

    @pl.when(jnp.logical_not(is_safe(l, acc)))
    def _():
        l[...] = jnp.zeros(l.shape, F32)
        acc[...] = jnp.zeros(acc.shape, F32)
        sweep(slow_block)


def state_specs():
    return [
        pl.BlockSpec((pl.squeezed, 2, 8, 1024), lambda i: (i, 0, 0, 0)),
        pl.BlockSpec((pl.squeezed, 2, 8, 1024), lambda i: (i, 0, 0, 0)),
        pl.BlockSpec((pl.squeezed, 2, 128, 1024), lambda i: (i, 0, 0, 0)),
    ]


def attend_cached(counts, queries, cache, name):
    slot_rows = cache[0].shape[2]
    total = 8 * slot_rows
    rows = queries[0].shape[0]
    chunks = len(queries)
    smem = pl.BlockSpec(memory_space=pltpu.SMEM)
    return pl.pallas_call(
        functools.partial(cached_kernel, slot_rows=slot_rows, chunks=chunks),
        grid=(chunks,),
        in_specs=[smem] + [pl.BlockSpec(memory_space=pl.ANY)] * (chunks + 3),
        out_specs=state_specs(),
        out_shape=[
            jax.ShapeDtypeStruct((chunks, 2, 8, 1024), F32),
            jax.ShapeDtypeStruct((chunks, 2, 8, 1024), F32),
            jax.ShapeDtypeStruct((chunks, 2, 128, 1024), F32),
        ],
        scratch_shapes=[
            pltpu.VMEM((total, 256), BF16),
            pltpu.VMEM((total, 256), BF16),
            pltpu.VMEM((256, total), BF16),
            pltpu.VMEM((chunks, rows, 2048), BF16),
            pltpu.VMEM((2, 1024, 128), BF16),
            pltpu.SemaphoreType.DMA((16 + chunks,)),
        ],
        compiler_params=pltpu.CompilerParams(vmem_limit_bytes=ROOMY_LIMIT),
        cost_estimate=pl.CostEstimate(flops=1000, bytes_accessed=1000, transcendentals=0),
        name=name,
    )(counts, *queries, *cache)


def fresh_kernel(*rest, chunks):
    queries, rest = rest[: len(chunks)], rest[len(chunks) :]
    states, rest = rest[: 3 * len(chunks)], rest[3 * len(chunks) :]
    parts, rest = rest[:8], rest[8:]
    outs, rest = rest[: len(chunks)], rest[len(chunks) :]
    keys, values_t, q_all, qs, bias, m, l, acc, sem = rest
    step = pl.program_id(0)
    first = step == 0
    chunk = jnp.int32(chunks[0])
    for i in range(1, len(chunks)):
        chunk = jnp.where(step == i, chunks[i], chunk)
    y, x, z, core = place()
    copies = [[], [], [], []]
    for n in range(8):
        side, k = n // 4, n % 4
        for xo in range(2):
            stacked, x1, x3, two = parts[side * 4 : side * 4 + 4]
            ref = (stacked.at[0], stacked.at[1], stacked.at[2], x1, two.at[0], two.at[1], stacked.at[3], x3)[k * 2 + xo]
            x_from = (x + xo) % 2
            at_p = side * 1024 + (xo * 4 + k) * 128
            at_s = pl.multiple_of(2048 + side * 1024 + (x_from * 4 + k) * 128, 128)
            c = (n * 2 + xo) * 4
            copies[side] += [
                pltpu.make_async_copy(ref.at[0:128, :], keys.at[at_p : at_p + 128, :], sem.at[c]),
                pltpu.make_async_copy(ref.at[256:512, 0:128], values_t.at[:, at_p : at_p + 128], sem.at[c + 1]),
            ]
            copies[2 + side] += [
                pltpu.make_async_copy(ref.at[128:256, :], keys.at[pl.ds(at_s, 128), :], sem.at[c + 2]),
                pltpu.make_async_copy(ref.at[256:512, 128:256], values_t.at[:, pl.ds(at_s, 128)], sem.at[c + 3]),
            ]
    query_copies = [pltpu.make_async_copy(q, q_all.at[i], sem.at[64 + i]) for i, q in enumerate(queries)]

    @pl.when(first)
    def _():
        for group in [query_copies] + copies:
            for c in group:
                c.start()

    for i, copy in enumerate(query_copies):

        @pl.when(step == i)
        def _(copy=copy):
            copy.wait()

    stack_queries(q_all.at[step], qs)

    def load_state():
        for i in range(len(chunks)):

            @pl.when(step == i)
            def _(i=i):
                for ref, source in zip((m, l, acc), states[3 * i : 3 * i + 3]):
                    ref[...] = source[0]

    load_state()
    block_y = y ^ chunk
    row = lax.broadcasted_iota(jnp.int32, (2048, 128), 0)
    lane = lax.broadcasted_iota(jnp.int32, (2048, 128), 1)
    key_core = jnp.where(row < 1024, core, 1 - core)
    key_z = z ^ ((row // 128) % 4)
    key_pos = 1024 * ((row // 512) % 2) + 256 * key_z + 128 * key_core + row % 128
    query_pos = 1024 * x + 256 * z + 128 * core + lane
    hidden = jnp.logical_and(y == block_y, key_pos > query_pos)
    bias[0:1024, :] = jnp.zeros((1024, 128), F32)
    bias[1024:3072, :] = jnp.where(hidden, -jnp.inf, 0.0)
    count = jnp.where(y <= block_y, 4, 2)

    def sweep(block, wait):
        def body(i, carry):
            if wait:
                for g in range(4):

                    @pl.when(jnp.logical_and(first, i == g))
                    def _(g=g):
                        for c in copies[g]:
                            c.wait()

            start = pl.multiple_of(i * 1024, 1024)
            b = bias[pl.ds(pl.multiple_of(jnp.maximum(i - 1, 0) * 1024, 1024), 1024), :]
            for j in range(2):
                k = head_rows(keys, start, 1024, j)
                vt = values_t[j * 128 : (j + 1) * 128, pl.ds(start, 1024)]
                block(j, k, vt, qs, m, l, acc, b)
            return carry

        lax.fori_loop(0, count, body, 0)

    sweep(fast_block, True)

    @pl.when(jnp.logical_and(first, count == 2))
    def _():
        for g in (2, 3):
            for c in copies[g]:
                c.wait()

    @pl.when(jnp.logical_not(is_safe(l, acc)))
    def _():
        load_state()
        sweep(slow_block, False)

    for i, out in enumerate(outs):

        @pl.when(step == i)
        def _(out=out):
            for j in range(2):
                total = jnp.sum(l[j], axis=0, keepdims=True)
                out[j, 0:128, :] = (acc[j] * (1.0 / total)).astype(out.dtype)
                lse = jnp.broadcast_to(m[j, 0:1, :] + jnp.log(total) * math.log2(math.e), (16, 1024))
                if out.dtype == BF16:
                    high = lse.astype(BF16).astype(F32)
                    mid = (lse - high).astype(BF16).astype(F32)
                    low = lse - high - mid
                    line = lax.broadcasted_iota(jnp.int32, (16, 1024), 0)
                    lse = jnp.where(line == 0, high, jnp.where(line == 1, mid, low))
                out[j, 128:144, :] = lse.astype(out.dtype)


def state_at(i):
    return [
        pl.BlockSpec((1, 2, 8, 1024), lambda _: (i, 0, 0, 0)),
        pl.BlockSpec((1, 2, 8, 1024), lambda _: (i, 0, 0, 0)),
        pl.BlockSpec((1, 2, 128, 1024), lambda _: (i, 0, 0, 0)),
    ]


def attend_fresh(chunks, queries, states, parts, dtype):
    whole = pl.BlockSpec(memory_space=pltpu.VMEM)
    anywhere = pl.BlockSpec(memory_space=pl.ANY)
    n = len(chunks)
    return pl.pallas_call(
        functools.partial(fresh_kernel, chunks=chunks),
        grid=(n,),
        in_specs=[anywhere] * n + [spec for _, i in states for spec in state_at(i)] + [anywhere] * 8,
        out_specs=[whole] * n,
        out_shape=[jax.ShapeDtypeStruct((2, 144, 1024), dtype)] * n,
        scratch_shapes=[
            pltpu.VMEM((4096, 256), BF16),
            pltpu.VMEM((256, 4096), BF16),
            pltpu.VMEM((n, 128, 2048), BF16),
            pltpu.VMEM((2, 1024, 128), BF16),
            pltpu.VMEM((3072, 128), F32),
            pltpu.VMEM((2, 8, 1024), F32),
            pltpu.VMEM((2, 8, 1024), F32),
            pltpu.VMEM((2, 128, 1024), F32),
            pltpu.SemaphoreType.DMA((64 + n,)),
        ],
        compiler_params=pltpu.CompilerParams(vmem_limit_bytes=VMEM_LIMIT),
        cost_estimate=pl.CostEstimate(flops=1000, bytes_accessed=1000, transcendentals=0),
        name="attend_fresh_" + "".join(str(c) for c in chunks),
    )(*queries, *[array for state, _ in states for array in state], *parts)


def merge_kernel(own, one, two, three, out):
    parts = (own, one, two, three)
    sizes = [own[128:129, :]]
    for ref in parts[1:]:
        tail = ref[128:144, :].astype(F32)
        sizes.append(tail[0:1] + tail[1:2] + tail[2:3])
    top = functools.reduce(jnp.maximum, sizes)
    shares = [jnp.exp2(size - top) for size in sizes]
    inverse = 1.0 / functools.reduce(jnp.add, shares)
    mixed = functools.reduce(
        jnp.add, [ref[0:128, :].astype(F32) * (share * inverse) for ref, share in zip(parts, shares)]
    )
    mixed = mixed.astype(BF16)
    for g in range(mixed.shape[1] // 128):
        out[:, g * 128 : (g + 1) * 128] = jnp.transpose(mixed[:, g * 128 : (g + 1) * 128])


def merge(parts):
    width = 1024
    return pl.pallas_call(
        merge_kernel,
        grid=(2048 // width,),
        in_specs=[pl.BlockSpec((pl.squeezed, 144, width), lambda i: (i, 0, 0))] * 4,
        out_specs=pl.BlockSpec((128, width), lambda i: (0, i)),
        out_shape=jax.ShapeDtypeStruct((128, 2048), BF16),
        compiler_params=pltpu.CompilerParams(vmem_limit_bytes=VMEM_LIMIT),
        cost_estimate=pl.CostEstimate(flops=1000, bytes_accessed=1000, transcendentals=0),
        name="merge",
    )(*parts)


def along_y(array, k):
    pairs = [(2 * y + x, 2 * (y ^ k) + x) for y in range(4) for x in range(2)]
    return lax.ppermute(array, "store", pairs)


def along_z(array, k):
    return lax.ppermute(array, "ctx", [(i, i ^ (2 * k)) for i in range(8)])


def swap_x(array):
    return lax.ppermute(array, "store", [(i, i ^ 1) for i in range(8)])


def swap_cores(array):
    return lax.ppermute(array, "ctx", [(i, i ^ 1) for i in range(8)])


def swap_heads(array):
    return lax.ppermute(array, "head", [(0, 1), (1, 0)])


def after(arrays, *others):
    return lax.optimization_barrier((tuple(arrays), others))[0]


def per_device(queries, suffix_hidden, prefix_hidden, kv_cache, counts, w_key, w_value):
    core = lax.axis_index("ctx") % 2
    own, other = project(prefix_hidden, suffix_hidden, w_key, w_value)
    received = swap_heads(other)
    half = lax.dynamic_slice(kv_cache, (2 * core, 0, 0, 0), (2,) + kv_cache.shape[1:])
    same = swap_x(half)
    q1, q3 = along_y(queries, 1), along_y(queries, 3)
    received, q1, q3, same = lax.optimization_barrier((received, q1, q3, same))
    payload = combine(own, received)

    late, same = after([queries, same], payload)
    by_x = swap_x(payload)
    z1, z3 = along_z(payload, 1), along_z(payload, 3)
    q2, swapped = along_y(late, 2), swap_cores(same)
    cache = (kv_cache, same, swapped)
    (q0,) = after([queries], payload)
    state_01 = attend_cached(counts, [q0, q1], cache, "cached_01")

    by_x, z1, z3, q2 = after([by_x, z1, z3, q2], *state_01)
    x1, x3 = along_z(by_x, 1), along_z(by_x, 3)
    near_a = jnp.stack([payload, by_x, z1, z3])
    two_z = along_z(near_a[0:2], 2)
    far_a = swap_cores(near_a)
    q2, q3 = after([q2, q3], near_a)
    state_23 = attend_cached(counts, [q2, q3], cache, "cached_23")
    tail = after([x1, x3, two_z], *state_23)
    parts = [near_a, *tail, far_a] + [swap_cores(part) for part in tail]

    (part_2,) = attend_fresh((2,), [q2], [(state_23, 0)], parts, BF16)
    two = along_y(part_2, 2)
    q1, q3 = after([q1, q3], part_2)
    part_1, part_3 = attend_fresh((1, 3), [q1, q3], [(state_01, 1), (state_23, 1)], parts, BF16)
    back_1, back_3 = along_y(part_1, 1), along_y(part_3, 3)
    (q0,) = after([queries], part_1, two)
    (mine,) = attend_fresh((0,), [q0], [(state_01, 0)], parts, F32)
    return merge([mine, back_1, two, back_3])


def solution(mesh):
    return jax.shard_map(
        per_device,
        mesh=mesh,
        in_specs=(
            P(("store", "ctx"), "head"),
            P(("store", "ctx"), "head"),
            P(("store", "ctx"), "head"),
            P("store", None, None, "head"),
            P(),
            P("head", None),
            P("head", None),
        ),
        out_specs=P(("store", "ctx"), "head"),
        check_vma=False,
    )
```
